256 devices in a mesh: outer: 32 (over y, z), inner: 8 (over x, core).
Axes of the slice: x: 4, y: 4, z: 8, core: 2. Of those that a mesh axis runs over, the one named last changes fastest.
Arguments:
- embeddings: bfloat16 [32768, 1536], P(('outer', 'inner')), may hold values from -6 to 6
- fine_centroids: bfloat16 [8192, 1536], P('inner'), may hold values from -6 to 6
- coarse_centroids: bfloat16 [1024, 1536], replicated, may hold values from -6 to 6
Outputs:
- new_fine: bfloat16 [8192, 1536], P('inner')
- new_coarse: bfloat16 [1024, 1536], P('inner')
The draws below stay inside these ranges and needn't reach their ends.
All inputs are finite; a program needn't handle non-finite values.
Results may differ from the reference program's by a relative error of at most 0.007.
Values may be sent and summed in bfloat16 or wider, within the bound.
No kernel may reach another device: no remote copies, remote signals or barrier semaphores. Data moves between devices by JAX's collectives and lax.ppermute only.
A program may use at most 128 MiB of HBM per device.

```python
import math
import jax
import jax.numpy as jnp
from jax import lax

D = 1536
FINE = 8192
COARSE = 1024
ROWS = 32768


def centroid_base(key):
    return jax.random.normal(jax.random.fold_in(key, 101), (FINE, D), jnp.float32)


def draw_fine_centroids(key, part):
    normal_base = centroid_base(key)
    values = jnp.clip(normal_base, -6.0, 6.0)
    return values.astype(jnp.bfloat16)


def draw_embeddings(key, part):
    key = jax.random.fold_in(key, 2)
    key_values = jax.random.fold_in(key, 1)
    values = jnp.clip(jax.random.normal(key_values, (ROWS, D), jnp.float32), -6.0, 6.0)
    return values.astype(jnp.bfloat16)


def draw_coarse_centroids(key, part):
    key = jax.random.fold_in(key, 3)
    key_values = jax.random.fold_in(key, 0)
    values = jnp.clip(jax.random.normal(key_values, (COARSE, D), jnp.float32), -6.0, 6.0)
    return values.astype(jnp.bfloat16)


def setup_inputs(seed: int = 0) -> dict:
    arg_keys = jax.random.split(jax.random.key(seed), 4)
    embeddings = draw_embeddings(jax.random.fold_in(arg_keys[3], 71), 0)
    fine_centroids = draw_fine_centroids(jax.random.fold_in(arg_keys[3], 71), 0)
    coarse_centroids = draw_coarse_centroids(jax.random.fold_in(arg_keys[3], 71), 0)
    return dict(embeddings=embeddings, fine_centroids=fine_centroids, coarse_centroids=coarse_centroids)


def soft_responsibility(scores):
    row_top = lax.optimization_barrier(jnp.max(scores, axis=1, keepdims=True))
    weights = jnp.exp(scores - row_top)
    return (weights / lax.optimization_barrier(jnp.sum(weights, axis=1, keepdims=True))).astype(jnp.bfloat16)

def soft_level(points, centers):
    row_count = points.shape[0]
    block_rows = math.gcd(row_count, 1024)
    score_scale = 4.0 / math.sqrt(points.shape[1])
    blocks = points.reshape(row_count // block_rows, block_rows, points.shape[1])

    def accumulate(totals, row_block):
        weighted, total_mass = totals
        scores = lax.dot_general(row_block, centers, (((1,), (1,)), ((), ())), preferred_element_type=jnp.float32) * score_scale
        weights_bf = soft_responsibility(scores)
        weighted = weighted + lax.dot_general(weights_bf, row_block, (((0,), (0,)), ((), ())), preferred_element_type=jnp.float32)
        total_mass = total_mass + lax.optimization_barrier(jnp.sum(weights_bf.astype(jnp.float32), axis=0))
        return ((weighted, total_mass), None)
    initial = (jnp.zeros((centers.shape[0], points.shape[1]), jnp.float32), jnp.zeros((centers.shape[0],), jnp.float32))
    (weighted, total_mass), _ = lax.scan(accumulate, initial, blocks)
    return (weighted / jnp.maximum(total_mass, 1.0)[:, None]).astype(jnp.bfloat16)

def reference(embeddings, fine_centroids, coarse_centroids):
    return (soft_level(embeddings, fine_centroids), soft_level(fine_centroids, coarse_centroids))
```

```python
import functools
import math

import jax
import jax.numpy as jnp
import numpy as np
from jax import lax
from jax.experimental import pallas as pl
from jax.experimental.pallas import tpu as pltpu
from jax.sharding import Mesh, PartitionSpec as P

D = 1536
ROWS = 128
BLOCK = 32
TILE = 256
EXTRA = 16
NA = 960 // 128 * 128
NB = D - NA
SCALE = 4.0 / math.sqrt(D)
BF16, F32 = jnp.bfloat16, jnp.float32
ROW_DOT = (((1,), (1,)), ((), ()))

Y_BITS = ((0, 0), (1, 0), (1, 1), (0, 1))
Z_BITS = tuple((g & 1, (g >> 1) & 1, (g >> 2) & 1) for g in (z ^ (z >> 1) for z in range(8)))


def label(y, z, c):
    h, g = Y_BITS[(y - c) % 4], Z_BITS[(z - c) % 8]
    return h[0] << 4 | h[1] << 3 | g[0] << 2 | g[1] << 1 | g[2]


def flip_pairs(bit):
    pairs = []
    for c in range(2):
        where = {label(y, z, c): (y * 8 + z) * 2 + c for y in range(4) for z in range(8)}
        pairs += [(where[k], where[k ^ (1 << bit)]) for k in where]
    return sorted(pairs)


FLIPS = {bit: flip_pairs(bit) for bit in range(5)}


def owner_tables():
    owner = np.zeros((4, 8, 2, 32), np.int32)
    place = np.zeros((4, 8, 2, 32), np.int32)
    for c in range(2):
        block = {label(y, z, c): y * 8 + z for y in range(4) for z in range(8)}
        for y in range(4):
            for z in range(8):
                for p in range(32):
                    b = block[p ^ label(y, z, c)]
                    owner[y, z, c, p] = b
                    place[y, z, c, b] = p
    return np.stack([owner.reshape(64, 32), place.reshape(64, 32)], 1)


TABLES = owner_tables()
COARSE_TABLE = np.array(
    [[(x + r) % 4 * 2 + (c ^ d) for r in range(4) for d in range(2)] for x in range(4) for c in range(2)], np.int32
)


def flip(x, bit):
    return lax.ppermute(x, ("y", "z", "c"), FLIPS[bit])


def from_x(x, k):
    return lax.ppermute(x, "x", [((i + k) % 4, i) for i in range(4)])


def swap_core(x):
    return lax.ppermute(x, "c", [(0, 1), (1, 0)])


def order_kernel(block, table, src, dst, sems):
    copies = []
    for p in range(src.shape[0] // block):
        rows = pl.ds(pl.multiple_of(table[p] * block, block), block)
        copies.append(pltpu.make_async_copy(src.at[rows], dst.at[pl.ds(p * block, block)], sems.at[p]))
        copies[-1].start()
    for copy in copies:
        copy.wait()


def in_order(table, x, block):
    return pl.pallas_call(
        functools.partial(order_kernel, block),
        out_shape=jax.ShapeDtypeStruct(x.shape, x.dtype),
        in_specs=[pl.BlockSpec(memory_space=pltpu.SMEM), pl.BlockSpec(memory_space=pl.ANY)],
        out_specs=pl.BlockSpec(memory_space=pltpu.VMEM),
        scratch_shapes=[pltpu.SemaphoreType.DMA((x.shape[0] // block,))],
        compiler_params=pltpu.CompilerParams(vmem_limit_bytes=8 << 20),
        cost_estimate=pl.CostEstimate(flops=0, bytes_accessed=2 * x.size * 2, transcendentals=0),
        name="order_centroids",
    )(table, x)


def finish_kernel(owner, a_own, a_got, b_own, b_got, out, sems):
    copies = []
    for p in range(32):
        py, pz = p // 8, p % 8
        rows = pl.ds(pl.multiple_of(owner[p] * BLOCK, BLOCK), BLOCK)
        a = a_own if p < 16 else a_got
        b = b_own if pz < 4 else b_got
        from_a = a.at[pl.ds(p % 16 * BLOCK, BLOCK)]
        from_b = b.at[pl.ds((py * 4 + pz % 4) * BLOCK, BLOCK)]
        copies.append(pltpu.make_async_copy(from_a, out.at[rows, pl.ds(0, NA)], sems.at[0, p]))
        copies.append(pltpu.make_async_copy(from_b, out.at[rows, pl.ds(NA, NB)], sems.at[1, p]))
        copies[-2].start()
        copies[-1].start()
    for copy in copies:
        copy.wait()


def finish(owner, a_own, a_got, b_own, b_got):
    return pl.pallas_call(
        finish_kernel,
        out_shape=jax.ShapeDtypeStruct((1024, D), BF16),
        in_specs=[pl.BlockSpec(memory_space=pltpu.SMEM)] + [pl.BlockSpec(memory_space=pl.ANY)] * 4,
        out_specs=pl.BlockSpec(memory_space=pltpu.VMEM),
        scratch_shapes=[pltpu.SemaphoreType.DMA((2, 32))],
        compiler_params=pltpu.CompilerParams(vmem_limit_bytes=8 << 20),
        cost_estimate=pl.CostEstimate(flops=0, bytes_accessed=4 * 1024 * D, transcendentals=0),
        name="finish_fine",
    )(owner, a_own, a_got, b_own, b_got)


def score_kernel(e0, e1, f, p_ref, top_ref, stat_ref, top_acc, sum_acc):
    t = pl.program_id(0)
    rows = jnp.concatenate([e0[...], e1[...]], axis=0)
    s = lax.dot_general(f[...], rows, ROW_DOT, preferred_element_type=F32)
    top = jnp.max(s, axis=0, keepdims=True)
    p = jnp.exp((s - top) * SCALE)
    p_ref[...] = p
    total = jnp.sum(p, axis=0, keepdims=True)
    top_ref[pl.ds(t, 1), :] = top

    @pl.when(t == 0)
    def _():
        top_acc[...] = top
        sum_acc[...] = total

    @pl.when(t > 0)
    def _():
        old = top_acc[...]
        new = jnp.maximum(old, top)
        sum_acc[...] = sum_acc[...] * jnp.exp((old - new) * SCALE) + total * jnp.exp((top - new) * SCALE)
        top_acc[...] = new

    @pl.when(t == 3)
    def _():
        m, l = top_acc[...], sum_acc[...]
        stat_ref[...] = jnp.concatenate([m[:, :ROWS], m[:, ROWS:], l[:, :ROWS], l[:, ROWS:]], axis=0)


def scores(e0, e1, f):
    whole = lambda *shape: pl.BlockSpec(shape, lambda t: (0,) * len(shape))
    return pl.pallas_call(
        score_kernel,
        grid=(4,),
        in_specs=[whole(ROWS, D), whole(ROWS, D), pl.BlockSpec((TILE, D), lambda t: (t, 0))],
        out_specs=[pl.BlockSpec((TILE, 2 * ROWS), lambda t: (t, 0)), whole(4, 2 * ROWS), whole(4, ROWS)],
        out_shape=[
            jax.ShapeDtypeStruct((1024, 2 * ROWS), F32),
            jax.ShapeDtypeStruct((4, 2 * ROWS), F32),
            jax.ShapeDtypeStruct((4, ROWS), F32),
        ],
        scratch_shapes=[pltpu.VMEM((1, 2 * ROWS), F32), pltpu.VMEM((1, 2 * ROWS), F32)],
        compiler_params=pltpu.CompilerParams(vmem_limit_bytes=16 << 20),
        cost_estimate=pl.CostEstimate(flops=2 * 1024 * 256 * D, bytes_accessed=6 << 20, transcendentals=1 << 18),
        name="fine_scores",
    )(e0, e1, f)


def two_rows(v):
    high = v.astype(BF16)
    low = (v - high.astype(F32)).astype(BF16)
    return jnp.concatenate([high, low, jnp.zeros((EXTRA - 2, v.shape[1]), BF16)], axis=0)


def sums_kernel(place, *refs):
    es, ps, tops, stats = refs[0:8], refs[8:12], refs[12:16], refs[16]
    a_send, a_keep, b_send, b_keep, m_keep, all_top, all_sum = refs[17:]
    t = pl.program_id(0)
    tile = lax.rem(t + 2, 4)

    @pl.when(t == 0)
    def _():
        x, c = place[0], place[1]
        for r in range(4):
            for d in range(2):
                ms, ls = [], []
                for src in range(8):
                    sr = lax.rem(x + (r + 4 - src // 2), 4)
                    sd = jnp.bitwise_xor(c, d ^ (src % 2))
                    at = sr * 4 + sd
                    ms.append(stats[src, pl.ds(at, 1), :])
                    ls.append(stats[src, pl.ds(at + 2, 1), :])
                top = ms[0]
                for m in ms[1:]:
                    top = jnp.maximum(top, m)
                total = jnp.zeros_like(top)
                for m, l in zip(ms, ls):
                    total = total + l * jnp.exp((m - top) * SCALE)
                all_top[pl.ds(r, 1), pl.ds(d * ROWS, ROWS)] = top
                all_sum[pl.ds(r, 1), pl.ds(d * ROWS, ROWS)] = total

    ones = jnp.ones((8, 2 * ROWS), BF16)
    out = jnp.zeros((TILE, D), F32)
    weight = jnp.zeros((8, TILE), F32)
    for r in range(4):
        top, total = all_top[pl.ds(r, 1), :], all_sum[pl.ds(r, 1), :]
        factor = jnp.exp((tops[r][pl.ds(tile, 1), :] - top) * SCALE) / total
        w = (ps[r][...] * factor).astype(BF16)
        rows = jnp.concatenate([es[2 * r][...], es[2 * r + 1][...]], axis=0)
        out = out + jnp.dot(w, rows, preferred_element_type=F32)
        weight = weight + lax.dot_general(ones, w, ROW_DOT, preferred_element_type=F32)
    weight = weight[:1, :]

    for i in range(2):

        @pl.when(t == i)
        def _():
            a_send[i * TILE : (i + 1) * TILE, :] = out[:, :NA].astype(BF16)
            a_send[512:, i * TILE : (i + 1) * TILE] = two_rows(weight)

        @pl.when(t == 2 + i)
        def _():
            m_keep[:, i * TILE : (i + 1) * TILE] = weight

    @pl.when(t == 0)
    def _():
        a_send[512:, 512:] = jnp.zeros((EXTRA, NA - 512), BF16)

    @pl.when(t >= 2)
    def _():
        a_keep[...] = out[:, :NA]

    b_keep[...] = out[: TILE // 2, NA:]
    b_send[...] = out[TILE // 2 :, NA:].astype(BF16)


def sums(place, es, ps, tops, stats):
    whole = lambda *shape: pl.BlockSpec(shape, lambda t, s: (0,) * len(shape))
    tile = lambda t: lax.rem(t + 2, 4)
    return pl.pallas_call(
        sums_kernel,
        grid_spec=pltpu.PrefetchScalarGridSpec(
            num_scalar_prefetch=1,
            grid=(4,),
            in_specs=[whole(ROWS, D)] * 8
            + [pl.BlockSpec((TILE, 2 * ROWS), lambda t, s: (tile(t), 0))] * 4
            + [whole(4, 2 * ROWS)] * 4
            + [whole(8, 16, ROWS)],
            out_specs=[
                whole(512 + EXTRA, NA),
                pl.BlockSpec((TILE, NA), lambda t, s: (jnp.maximum(t - 2, 0), 0)),
                pl.BlockSpec((TILE // 2, NB), lambda t, s: (tile(t), 0)),
                pl.BlockSpec((TILE // 2, NB), lambda t, s: (tile(t), 0)),
                whole(1, 512),
            ],
            scratch_shapes=[pltpu.VMEM((4, 2 * ROWS), F32), pltpu.VMEM((4, 2 * ROWS), F32)],
        ),
        out_shape=[
            jax.ShapeDtypeStruct((512 + EXTRA, NA), BF16),
            jax.ShapeDtypeStruct((512, NA), F32),
            jax.ShapeDtypeStruct((512, NB), BF16),
            jax.ShapeDtypeStruct((512, NB), F32),
            jax.ShapeDtypeStruct((1, 512), F32),
        ],
        compiler_params=pltpu.CompilerParams(vmem_limit_bytes=24 << 20),
        cost_estimate=pl.CostEstimate(flops=2 * 1024 * 1024 * D, bytes_accessed=14 << 20, transcendentals=0),
        name="fine_sums",
    )(place, *es, *ps, *tops, stats)


def coarse_kernel(s, top, total, fine, keep, send, m_keep):
    w = (jnp.exp(s[...] - top[...]) / total[...]).astype(BF16)
    out = jnp.dot(w, fine[...], preferred_element_type=F32)
    weight = lax.dot_general(jnp.ones((8, 1024), BF16), w, ROW_DOT, preferred_element_type=F32)[:1, :]
    keep[0] = out[:128]
    send[0, :128] = out[128:].astype(BF16)
    send[0, 128:, :128] = two_rows(weight[:, 128:])
    send[0, 128:, 128:] = jnp.zeros((EXTRA, D - 128), BF16)
    m_keep[0] = weight[:, :128]


def coarse_sums(s, top, total, fine):
    whole = lambda *shape: pl.BlockSpec(shape, lambda r: (0,) * len(shape))
    row = lambda *shape: pl.BlockSpec((1, *shape), lambda r: (r, 0, 0))
    return pl.pallas_call(
        coarse_kernel,
        grid=(4,),
        in_specs=[pl.BlockSpec((256, 1024), lambda r: (r, 0)), whole(1, 1024), whole(1, 1024), whole(1024, D)],
        out_specs=[row(128, D), row(128 + EXTRA, D), row(1, 128)],
        out_shape=[
            jax.ShapeDtypeStruct((4, 128, D), F32),
            jax.ShapeDtypeStruct((4, 128 + EXTRA, D), BF16),
            jax.ShapeDtypeStruct((4, 1, 128), F32),
        ],
        compiler_params=pltpu.CompilerParams(vmem_limit_bytes=24 << 20),
        cost_estimate=pl.CostEstimate(flops=2 * 1024 * 1024 * D, bytes_accessed=12 << 20, transcendentals=1 << 20),
        name="coarse_sums",
    )(s, top, total, fine)


def split(v):
    high = lax.reduce_precision(v, 8, 7)
    return high, lax.reduce_precision(v - high, 8, 7)


def with_mass(total, mass):
    high, low = split(mass)
    rows = jnp.pad(jnp.stack([high, low]), ((0, EXTRA - 2), (0, total.shape[1] - mass.shape[0])))
    return jnp.concatenate([total, rows], axis=0).astype(BF16)


def coarse_scores(fine, ordered):
    s = lax.dot_general(ordered, fine, ROW_DOT, preferred_element_type=F32) * SCALE
    top = jnp.max(s, axis=0, keepdims=True)
    return s, top, jnp.sum(jnp.exp(s - top), axis=0, keepdims=True)


def coarse_rows(keep, send, m_keep):
    got = swap_core(send).astype(F32)
    total = keep + got[:, :128]
    mass = m_keep[:, 0] + got[:, 128, :128] + got[:, 129, :128]
    out, m = total[0], mass[0]
    for k in (1, 3, 2):
        block = lax.ppermute(with_mass(total[k], mass[k]), "x", [(i, (i + k) % 4) for i in range(4)]).astype(F32)
        out = out + block[:128]
        m = m + block[128, :128] + block[129, :128]
    return (out / jnp.maximum(m, 1.0)[:, None]).astype(BF16)


def shards(embeddings, fine, coarse):
    y, z, x, c = (lax.axis_index(a) for a in ("y", "z", "x", "c"))
    o = y * 8 + z
    tables = lax.dynamic_index_in_dim(jnp.asarray(TABLES), o * 2 + c, 0, keepdims=False)
    owner = tables[0]
    coarse_order = lax.dynamic_index_in_dim(jnp.asarray(COARSE_TABLE), x * 2 + c, 0, keepdims=False)

    got = {0: embeddings}
    for r in (1, 3, 2):
        got[r] = from_x(embeddings, r)
    pairs = {r: (got[r], swap_core(got[r])) for r in (0, 1, 3, 2)}
    ordered = in_order(owner, fine, BLOCK)
    c_scores = coarse_scores(fine, in_order(coarse_order, coarse, 128))
    ps, tops, stats = {}, {}, {}
    for r in (0, 1, 3, 2):
        ps[r], tops[r], stats[r] = scores(*pairs[r], ordered)
    stats = jnp.concatenate([stats[r] for r in range(4)], axis=0)
    stats = lax.all_to_all(jnp.broadcast_to(stats[None], (8, 16, ROWS)), ("x", "c"), 0, 0)
    es = [block for r in range(4) for block in pairs[r]]
    a_send, a_keep, b_send, b_keep, m_keep = sums(
        jnp.stack([x, c]), es, [ps[r] for r in range(4)], [tops[r] for r in range(4)], stats
    )
    c_scores, a_keep, b_keep = lax.optimization_barrier((c_scores, a_keep, b_keep))
    c_sums = coarse_sums(*c_scores, fine)

    rows = 512
    m_keep = m_keep[0]
    for bit in (4, 3, 2, 1, 0):
        got = flip(a_send, bit).astype(F32)
        total = a_keep + got[:rows]
        mass = m_keep + got[rows, :rows] + got[rows + 1, :rows]
        if bit:
            rows //= 2
            a_keep, m_keep = total[:rows], mass[:rows]
            a_send = with_mass(total[rows:], mass[rows:])
    mass = jnp.maximum(mass, 1.0)[:, None]
    a = (total / mass).astype(BF16)
    b_keep, b_send = b_keep.reshape(4, 4, BLOCK, NB), b_send.reshape(4, 4, BLOCK, NB)
    for bit in (2, 1, 0, 4, 3):
        total = b_keep + flip(b_send, bit).astype(F32)
        if bit in (2, 1):
            half = total.shape[1] // 2
            b_keep, b_send = total[:, :half], total[:, half:].astype(BF16)
        elif bit in (0, 4):
            half = total.shape[0] // 2
            b_keep, b_send = total[:half], total[half:].astype(BF16)
    b = (total.reshape(BLOCK, NB) / mass).astype(BF16)

    for bit in (0, 1, 2, 3):
        a = jnp.concatenate([a, flip(a, bit)], axis=0)
    a_got = flip(a, 4)
    b = b.reshape(1, 1, BLOCK, NB)
    for bit, axis in ((3, 0), (4, 0), (0, 1), (1, 1)):
        b = jnp.concatenate([b, flip(b, bit)], axis=axis)
    b_got = flip(b, 2)
    new_fine = finish(owner, a, a_got, b.reshape(512, NB), b_got.reshape(512, NB))
    return new_fine, coarse_rows(*c_sums)


def solution(mesh):
    torus = Mesh(mesh.devices.reshape(4, 8, 4, 2), ("y", "z", "x", "c"))
    return jax.shard_map(
        shards,
        mesh=torus,
        in_specs=(P(("y", "z", "x", "c"), None), P(("x", "c"), None), P()),
        out_specs=(P(("x", "c"), None), P(("x", "c"), None)),
        check_vma=False,
    )
```

```python
import functools
import math

import jax
import jax.numpy as jnp
import numpy as np
from jax import lax
from jax.experimental import pallas as pl
from jax.experimental.pallas import tpu as pltpu
from jax.sharding import Mesh, PartitionSpec as P

D = 1536
ROWS = 128
HALF = ROWS // 2
BLOCK = 32
TILE = 8 * BLOCK
EXTRA = 16
WIDE = D + 128
CALL_OF = ((0, 0), (1, 0), (2, 0), (1, 2 * ROWS))
FIRST_BLOCK = (0, 2, 6, 4)
SCALE = 4.0 / math.sqrt(D)
BF16, F32 = jnp.bfloat16, jnp.float32
ROW_DOT = (((1,), (1,)), ((), ()))

Z_PAIRS = ((1, 0, 3, 2, 5, 4, 7, 6), (7, 2, 1, 4, 3, 6, 5, 0), (3, 6, 5, 0, 7, 2, 1, 4))


def partner(step, z, c):
    return (Z_PAIRS[step][(z - c) % 8] + c) % 8


def order(step, z, c):
    if step == 2:
        return sorted((z, partner(2, z, c)))
    return order(step + 1, z, c) + order(step + 1, partner(step, z, c), c)


X_PAIRS = ((1, 0, 3, 2), (3, 2, 1, 0))


def x_partner(step, x, c):
    return (X_PAIRS[step][(x - c) % 4] + c) % 4


def x_order(step, x, c):
    if step == 2:
        return [x]
    return x_order(step + 1, x, c) + x_order(step + 1, x_partner(step, x, c), c)


X_ORDER = np.array(
    [
        x_order(0, x, c) + [x_order(0, x, 1 - c).index(i) for i in x_order(0, x, c)]
        for x in range(4)
        for c in range(2)
    ],
    np.int32,
)
Z_ORDER = np.array([order(0, z, c) for z in range(8) for c in range(2)], np.int32)


def exchange(x, step):
    return lax.ppermute(x, ("z", "c"), [(z * 2 + c, partner(step, z, c) * 2 + c) for z in range(8) for c in range(2)])


def x_exchange(v, step):
    return lax.ppermute(
        v, ("x", "c"), [(x * 2 + c, x_partner(step, x, c) * 2 + c) for x in range(4) for c in range(2)]
    )


def shift(x, axis, k):
    n = {"x": 4, "y": 4}[axis]
    return lax.ppermute(x, axis, [(i, (i + k) % n) for i in range(n)])


def swap_core(x):
    return lax.ppermute(x, "c", [(0, 1), (1, 0)])


def ring_gather(h0, h1, axis, first=None):
    below0, above1 = shift(h0, axis, 1), shift(h1, axis, -1)
    below1, above0 = shift(h1, axis, 1), shift(h0, axis, -1)
    far = shift(below0, axis, 1), shift(above1, axis, -1)
    if first is not None:
        below1, above0, first = lax.optimization_barrier((below1, above0, first))
    return (below0, below1), (above0, above1), far, first


def place_kernel(rs, place, *refs):
    parts, out, sems = refs[: len(rs)], refs[-2], refs[-1]
    copies = []
    for i, (part, (r, h)) in enumerate(zip(parts, rs)):
        for j in range(4):
            row = lax.rem(place[0] + r, 4) * TILE + place[4 + 4 * h + j] * BLOCK
            rows = out.at[pl.ds(pl.multiple_of(row, BLOCK), BLOCK)]
            copies.append(pltpu.make_async_copy(part.at[pl.ds(j * BLOCK, BLOCK)], rows, sems.at[4 * i + j]))
    for copy in copies:
        copy.start()
    for copy in copies:
        copy.wait()


def put_rows(place, parts, rs, to=None):
    whole = [pl.BlockSpec(memory_space=pltpu.VMEM)] * len(parts)
    return pl.pallas_call(
        functools.partial(place_kernel, rs),
        out_shape=jax.ShapeDtypeStruct((1024, D), BF16),
        in_specs=[pl.BlockSpec(memory_space=pltpu.SMEM)] + whole + [pl.BlockSpec(memory_space=pl.ANY)] * (to is not None),
        out_specs=pl.BlockSpec(memory_space=pl.ANY),
        scratch_shapes=[pltpu.SemaphoreType.DMA((4 * len(parts),))],
        input_output_aliases={} if to is None else {len(parts) + 1: 0},
        compiler_params=pltpu.CompilerParams(vmem_limit_bytes=16 << 20),
        cost_estimate=pl.CostEstimate(flops=0, bytes_accessed=4 * 128 * len(parts) * D, transcendentals=0),
        name="put_rows",
    )(place, *parts, *([] if to is None else [to]))


def score_kernel(n, others, *refs):
    es, f, stats = refs[:n], refs[n], refs[n + 1 : n + 1 + others]
    p_ref, top_ref, stat_ref, top_acc, sum_acc = refs[n + 1 + others :]
    t = pl.program_id(0)
    rows = jnp.concatenate([e[...] for e in es], axis=0)
    s = lax.dot_general(f[...], rows, ROW_DOT, preferred_element_type=F32)
    top = jnp.max(s, axis=0, keepdims=True)
    p = jnp.exp((s - top) * SCALE)
    p_ref[...] = p
    total = jnp.sum(p, axis=0, keepdims=True)

    @pl.when(t == 0)
    def _():
        top_ref[:1, :] = top
        top_acc[...] = top
        sum_acc[...] = total

    @pl.when(t == 1)
    def _():
        top_ref[1:, :] = top
        old = top_acc[...]
        new = jnp.maximum(old, top)
        l = sum_acc[...] * jnp.exp((old - new) * SCALE) + total * jnp.exp((top - new) * SCALE)
        stat = []
        for at in range(0, rows.shape[0], 256):
            for v in (new, l):
                stat += [v[:, at : at + ROWS], v[:, at + ROWS : at + 256]]
        stat = jnp.concatenate(stat, axis=0)
        if stats:
            own, near = stats
            stat = jnp.concatenate([own[...], near[:4, :], stat, near[4:, :]], axis=0)
            for i in range(8):
                stat_ref[i] = stat
        else:
            stat_ref[...] = stat


def scores(es, f, *stats):
    rows = sum(e.shape[0] for e in es)
    whole = lambda *shape: pl.BlockSpec(shape, lambda t: (0,) * len(shape))
    stat = (8, 16, ROWS) if stats else (rows // 64, ROWS)
    return pl.pallas_call(
        functools.partial(score_kernel, len(es), len(stats)),
        grid=(2,),
        in_specs=[whole(*e.shape) for e in es]
        + [pl.BlockSpec((512, D), lambda t: (t, 0))]
        + [whole(*v.shape) for v in stats],
        out_specs=[pl.BlockSpec((512, rows), lambda t: (t, 0)), whole(2, rows), whole(*stat)],
        out_shape=[
            jax.ShapeDtypeStruct((1024, rows), F32),
            jax.ShapeDtypeStruct((2, rows), F32),
            jax.ShapeDtypeStruct(stat, F32),
        ],
        scratch_shapes=[pltpu.VMEM((1, rows), F32), pltpu.VMEM((1, rows), F32)],
        compiler_params=pltpu.CompilerParams(vmem_limit_bytes=58 << 20),
        cost_estimate=pl.CostEstimate(flops=2 * 1024 * rows * D, bytes_accessed=6 << 20, transcendentals=1024 * rows),
        name="fine_scores",
    )(*es, f, *stats)


def find_factors(place, tops, stats, factors):
    x, c = place[1], place[2]
    for r in range(4):
        for d in range(2):
            ms, ls = [], []
            for src in range(8):
                sr = lax.rem(x + (r + 4 - src // 2), 4)
                sd = jnp.bitwise_xor(c, d ^ (src % 2))
                at = sr * 4 + sd
                ms.append(stats[src, pl.ds(at, 1), :])
                ls.append(stats[src, pl.ds(at + 2, 1), :])
            top = ms[0]
            for m in ms[1:]:
                top = jnp.maximum(top, m)
            total = jnp.zeros_like(top)
            for m, l in zip(ms, ls):
                total = total + l * jnp.exp((m - top) * SCALE)
            call, at = CALL_OF[r]
            at += d * ROWS
            to = (FIRST_BLOCK[r] + d) * ROWS
            factors[:, to : to + ROWS] = jnp.exp((tops[call][:, at : at + ROWS] - top) * SCALE) / total


def tile_sums(place, tile, factors, ps, es):
    out = jnp.zeros((TILE, D), F32)
    mass = jnp.zeros((TILE, 128), F32)
    at, k = 0, 0
    for p in ps:
        cols = p.shape[1]
        blocks = [p[pl.ds(pl.multiple_of(place[4 + j] * BLOCK, BLOCK), BLOCK), :] for j in range(8)]
        w = (jnp.concatenate(blocks, axis=0) * factors[pl.ds(tile // 2, 1), at : at + cols]).astype(BF16)
        rows = []
        while sum(e.shape[0] for e in rows) < cols:
            rows.append(es[k][...])
            k += 1
        out = out + jnp.dot(w, jnp.concatenate(rows, axis=0), preferred_element_type=F32)
        mass = mass + jnp.dot(w, jnp.ones((cols, 128), BF16), preferred_element_type=F32)
        at += cols
    return out, mass


def put_halves(out, mass, keep, keep_mass, send):
    keep[...] = out[:128]
    keep_mass[...] = mass[:128]
    send[:, :D] = out[128:].astype(BF16)
    high = mass[128:].astype(BF16).astype(F32)
    lane = lax.broadcasted_iota(jnp.int32, (128, 128), 1)
    send[:, D:] = jnp.where(lane < 64, high, mass[128:] - high).astype(BF16)


def far_kernel(n, place, *refs):
    es, ps, tops, stats = refs[:n], refs[n : n + 3], refs[n + 3 : n + 6], refs[n + 6]
    keep, keep_mass, send, factors = refs[n + 7 :]
    find_factors(place, tops, stats, factors)
    out, mass = tile_sums(place, lax.rem(place[0] + 2, 4), factors, ps, es)
    put_halves(out, mass, keep, keep_mass, send)


def rest_kernel(n, place, *refs):
    es, ps, factors = refs[:n], refs[n : n + 3], refs[n + 3]
    outs = refs[n + 4 :]
    t = pl.program_id(0)
    out, mass = tile_sums(place, rest_tile(t, place), factors, ps, es)
    for i in range(3):

        @pl.when(t == i)
        def _():
            put_halves(out, mass, *outs[3 * i : 3 * i + 3])


def rest_tile(t, place):
    return lax.rem(place[0] + jnp.where(t == 0, 1, jnp.where(t == 1, 3, 0)), 4)


def fine_sums(place, es, ps, tops, stats):
    whole = lambda *shape: pl.BlockSpec(shape, lambda t, s: (0,) * len(shape))
    halves = [
        jax.ShapeDtypeStruct((128, D), F32),
        jax.ShapeDtypeStruct((128, 128), F32),
        jax.ShapeDtypeStruct((128, WIDE), BF16),
    ]
    specs = [whole(*half.shape) for half in halves]
    params = pltpu.CompilerParams(vmem_limit_bytes=58 << 20)
    *far, factors = pl.pallas_call(
        functools.partial(far_kernel, len(es)),
        grid_spec=pltpu.PrefetchScalarGridSpec(
            num_scalar_prefetch=1,
            grid=(1,),
            in_specs=[whole(*e.shape) for e in es]
            + [pl.BlockSpec((TILE, p.shape[1]), lambda t, s: (lax.rem(s[0] + 2, 4), 0)) for p in ps]
            + [whole(*top.shape) for top in tops]
            + [whole(8, 16, ROWS)],
            out_specs=specs + [whole(2, 1024)],
        ),
        out_shape=halves + [jax.ShapeDtypeStruct((2, 1024), F32)],
        compiler_params=params,
        cost_estimate=pl.CostEstimate(flops=2 * 256 * 1024 * D, bytes_accessed=5 << 20, transcendentals=0),
        name="far_sums",
    )(place, *es, *ps, *tops, stats)
    rest = pl.pallas_call(
        functools.partial(rest_kernel, len(es)),
        grid_spec=pltpu.PrefetchScalarGridSpec(
            num_scalar_prefetch=1,
            grid=(3,),
            in_specs=[whole(*e.shape) for e in es]
            + [pl.BlockSpec((TILE, p.shape[1]), lambda t, s: (rest_tile(t, s), 0)) for p in ps]
            + [whole(2, 1024)],
            out_specs=specs * 3,
        ),
        out_shape=halves * 3,
        compiler_params=params,
        cost_estimate=pl.CostEstimate(flops=2 * 768 * 1024 * D, bytes_accessed=10 << 20, transcendentals=0),
        name="rest_sums",
    )(place, *es, *ps, factors)
    return far, rest[:3], rest[3:6], rest[6:]


def load(ref, at, n):
    if isinstance(ref, tuple):
        return ref[0][at : at + n, :], ref[1][at : at + n, :]
    mass = ref[at : at + n, D:].astype(F32)
    mass = mass[:, :1] + mass[:, 64:65]
    return ref[at : at + n, :D].astype(F32), jnp.broadcast_to(mass, (n, 128))


def add(a, b):
    return a[0] + b[0], a[1] + b[1]


def store(ref, v):
    sums, mass = v
    ref[:, :D] = sums.astype(BF16)
    high = mass.astype(BF16).astype(F32)
    lane = lax.broadcasted_iota(jnp.int32, mass.shape, 1)
    ref[:, D:] = jnp.where(lane < 64, high, mass - high).astype(BF16)


def far_step(keep, mass, got, low, high):
    for at, out in ((0, low), (64, high)):
        store(out, add(load((keep, mass), at, 64), load(got, at, 64)))


def side_step(first, keep, mass, got, far, out):
    for at in (0, 64):
        v = add(load((keep, mass), at, 64), load(got, at, 64))
        if at == first:
            v = add(v, load(far, 0, 64))
        store(out.at[pl.ds(at, 64)], v)


def own_step(keep, mass, got, up, down, sums, masses, send):
    for at in (0, 64):
        v = add(load((keep, mass), at, 64), load(got, at, 64))
        v = add(v, add(load(up, at, 64), load(down, at, 64)))
        if at:
            store(send, v)
        else:
            sums[...], masses[...] = v


def half_step(keep, mass, got, out):
    store(out, add(load((keep, mass), 0, 64), load(got, 0, 64)))


def last_step(own, got, out):
    sums, mass = add(load(own, 0, 64), load(got, 0, 64))
    out[...] = (sums / jnp.maximum(mass[:, :1], 1.0)).astype(BF16)


def step(kernel, args, outs):
    whole = pl.BlockSpec(memory_space=pltpu.VMEM)
    out = pl.pallas_call(
        kernel,
        in_specs=[whole] * len(args),
        out_specs=[whole] * len(outs),
        out_shape=[jax.ShapeDtypeStruct(shape, t) for shape, t in outs],
        compiler_params=pltpu.CompilerParams(vmem_limit_bytes=16 << 20),
        cost_estimate=pl.CostEstimate(flops=1 << 20, bytes_accessed=2 << 20, transcendentals=0),
        name="add_" + getattr(kernel, "func", kernel).__name__,
    )(*args)
    return out if len(out) > 1 else out[0]


def coarse_kernel(place, s, top, total, fine, keep, send, m_keep):
    w = (jnp.exp(s[...] - top[...]) / total[...]).astype(BF16)
    out = jnp.dot(w, fine[...], preferred_element_type=F32)
    weight = lax.dot_general(jnp.ones((8, 1024), BF16), w, ROW_DOT, preferred_element_type=F32)[:1, :]
    first = place[2] == 0
    keep[0] = jnp.where(first, out[:128], out[128:])
    send[0, :128] = jnp.where(first, out[128:], out[:128]).astype(BF16)
    m_keep[0] = jnp.where(first, weight[:, :128], weight[:, 128:])
    sent = jnp.where(first, weight[:, 128:], weight[:, :128])
    high = sent.astype(BF16)
    low = (sent - high.astype(F32)).astype(BF16)
    send[0, 128:, :256] = jnp.broadcast_to(jnp.concatenate([high, low], axis=1), (EXTRA, 256))
    send[0, 128:, 256:] = jnp.zeros((EXTRA, D - 256), BF16)


def coarse_sums(place, s, top, total, fine):
    whole = lambda *shape: pl.BlockSpec(shape, lambda r, p: (0,) * len(shape))
    row = lambda *shape: pl.BlockSpec((1, *shape), lambda r, p: (r, 0, 0))
    swapped = pl.BlockSpec((1, 128 + EXTRA, D), lambda r, p: (p[16 + r], 0, 0))
    return pl.pallas_call(
        coarse_kernel,
        grid_spec=pltpu.PrefetchScalarGridSpec(
            num_scalar_prefetch=1,
            grid=(4,),
            in_specs=[pl.BlockSpec((256, 1024), lambda r, p: (p[12 + r], 0))]
            + [whole(1, 1024), whole(1, 1024), whole(1024, D)],
            out_specs=[row(128, D), swapped, row(1, 128)],
        ),
        out_shape=[
            jax.ShapeDtypeStruct((4, 128, D), F32),
            jax.ShapeDtypeStruct((4, 128 + EXTRA, D), BF16),
            jax.ShapeDtypeStruct((4, 1, 128), F32),
        ],
        compiler_params=pltpu.CompilerParams(vmem_limit_bytes=24 << 20),
        cost_estimate=pl.CostEstimate(flops=2 * 1024 * 1024 * D, bytes_accessed=12 << 20, transcendentals=1 << 20),
        name="coarse_sums",
    )(place, s, top, total, fine)


def split(v):
    high = lax.reduce_precision(v, 8, 7)
    return high, lax.reduce_precision(v - high, 8, 7)


def with_mass(total, mass, extra=EXTRA):
    rows = jnp.concatenate(split(mass), axis=1)
    rows = jnp.pad(rows, ((0, extra - rows.shape[0]), (0, total.shape[1] - rows.shape[1])))
    return jnp.concatenate([total, rows], axis=0).astype(BF16)


def coarse_scores(fine, coarse):
    s = lax.dot_general(coarse, fine, ROW_DOT, preferred_element_type=F32) * SCALE
    top = jnp.max(s, axis=0, keepdims=True)
    return s, top, jnp.sum(jnp.exp(s - top), axis=0, keepdims=True)


def coarse_rows(keep, send, m_keep):
    got = swap_core(send).astype(F32)
    total = keep + got[:, :128]
    mass = m_keep[:, 0] + got[:, 128, :128] + got[:, 128, 128:256]
    for step, n in ((0, 2), (1, 1)):
        got = x_exchange(with_mass(total[n:].reshape(n * 128, D), mass[n:], 8), step).astype(F32)
        total = total[:n] + got[: n * 128].reshape(n, 128, D)
        mass = mass[:n] + got[n * 128 : n * 128 + n, :128] + got[n * 128 : n * 128 + n, 128:256]
    return (total[0] / jnp.maximum(mass[0], 1.0)[:, None]).astype(BF16)


def shards(embeddings, fine, coarse):
    y, z, x, c = (lax.axis_index(a) for a in ("y", "z", "x", "c"))
    z_order = lax.dynamic_index_in_dim(jnp.asarray(Z_ORDER), z * 2 + c, 0, keepdims=False)
    x_places = lax.dynamic_index_in_dim(jnp.asarray(X_ORDER), x * 2 + c, 0, keepdims=False)
    place = jnp.concatenate([jnp.stack([y, x, c, z]), z_order, x_places])

    mine = [embeddings, swap_core(embeddings)]
    own = scores(mine, fine)
    below, above, far, own = ring_gather(embeddings[:HALF], embeddings[HALF:], "x", own)
    near = [*above, *map(swap_core, above), *below, *map(swap_core, below)]
    far = [*far, *map(swap_core, far)]
    calls = [own, scores(near, fine)]
    calls.append(scores(far, fine, calls[0][2], calls[1][2]))
    stats = lax.all_to_all(calls[2][2], ("x", "c"), 0, 0)
    far, up, down, own = fine_sums(
        place, [*mine, *near, *far], [call[0] for call in calls], [call[1] for call in calls], stats
    )

    sent = lambda n: ((n, WIDE), BF16)
    got = exchange(far[2], 0)
    rest, got = lax.optimization_barrier(((up, down, own), got))
    up, down, own = rest
    got_up, got_down, got_own = (exchange(v[2], 0) for v in rest)
    far0, far1 = step(far_step, [far[0], far[1], got], [sent(64), sent(64)])
    far0, far1 = shift(far0, "y", 1), shift(far1, "y", -1)
    up = step(functools.partial(side_step, 0), [up[0], up[1], got_up, far0], [sent(128)])
    down = step(functools.partial(side_step, 64), [down[0], down[1], got_down, far1], [sent(128)])
    up, down, got_own, coarse = lax.optimization_barrier((up, down, got_own, coarse))
    c_sums = coarse_sums(place, *coarse_scores(fine, coarse), fine)
    up, down = shift(up, "y", 1), shift(down, "y", -1)
    up, down, c_sums = lax.optimization_barrier((up, down, c_sums))
    sums, masses, send = step(
        own_step, [own[0], own[1], got_own, up, down], [((64, D), F32), ((64, 128), F32), sent(64)]
    )

    own = step(half_step, [sums, masses, exchange(send, 1)], [sent(64)])
    a = step(last_step, [own, exchange(own, 2)], [((64, D), BF16)])

    a0 = jnp.concatenate([a, exchange(a, 1)], axis=0)
    a1 = exchange(a0, 0)
    below0, above0 = shift(a0, "y", 1), shift(a0, "y", -1)
    a1, below0, above0 = lax.optimization_barrier((a1, below0, above0))
    above1, below1 = shift(a1, "y", -1), shift(a1, "y", 1)
    far0, far1 = shift(below0, "y", 1), shift(above1, "y", -1)
    new_fine = put_rows(place, [a0, a1, above0, below0], [(0, 0), (0, 1), (1, 0), (3, 0)])
    new_coarse = coarse_rows(*c_sums)
    far1, new_coarse, new_fine = lax.optimization_barrier((far1, new_coarse, new_fine))
    new_fine = put_rows(place, [above1, far0, far1, below1], [(1, 1), (2, 0), (2, 1), (3, 1)], new_fine)
    return new_fine, new_coarse


def solution(mesh):
    torus = Mesh(mesh.devices.reshape(4, 8, 4, 2), ("y", "z", "x", "c"))
    return jax.shard_map(
        shards,
        mesh=torus,
        in_specs=(P(("y", "z", "x", "c"), None), P(("x", "c"), None), P()),
        out_specs=(P(("x", "c"), None), P(("x", "c"), None)),
        check_vma=False,
    )
```

```python
import functools
import math

import jax
import jax.numpy as jnp
import numpy as np
from jax import lax
from jax.experimental import pallas as pl
from jax.experimental.pallas import tpu as pltpu
from jax.sharding import Mesh, PartitionSpec as P

D = 1536
ROWS = 128
HALF = ROWS // 2
BLOCK = 32
TILE = 8 * BLOCK
EXTRA = 16
WIDE = D + 128
CALL_OF = ((0, 0), (1, 0), (2, 0), (1, 2 * ROWS))
FIRST_BLOCK = (0, 2, 6, 4)
SCALE = 4.0 / math.sqrt(D)
BF16, F32 = jnp.bfloat16, jnp.float32
ROW_DOT = (((1,), (1,)), ((), ()))

Z_PAIRS = ((1, 0, 3, 2, 5, 4, 7, 6), (7, 2, 1, 4, 3, 6, 5, 0), (3, 6, 5, 0, 7, 2, 1, 4))


def partner(step, z, c):
    return (Z_PAIRS[step][(z - c) % 8] + c) % 8


def order(step, z, c):
    if step == 2:
        return sorted((z, partner(2, z, c)))
    return order(step + 1, z, c) + order(step + 1, partner(step, z, c), c)


X_PAIRS = ((1, 0, 3, 2), (3, 2, 1, 0))


def x_partner(step, x, c):
    return (X_PAIRS[step][(x - c) % 4] + c) % 4


def x_order(step, x, c):
    if step == 2:
        return [x]
    return x_order(step + 1, x, c) + x_order(step + 1, x_partner(step, x, c), c)


X_ORDER = np.array(
    [
        x_order(0, x, c) + [x_order(0, x, 1 - c).index(i) for i in x_order(0, x, c)]
        for x in range(4)
        for c in range(2)
    ],
    np.int32,
)
Z_ORDER = np.array([order(0, z, c) for z in range(8) for c in range(2)], np.int32)


def exchange(x, step):
    return lax.ppermute(x, ("z", "c"), [(z * 2 + c, partner(step, z, c) * 2 + c) for z in range(8) for c in range(2)])


def x_exchange(v, step):
    return lax.ppermute(
        v, ("x", "c"), [(x * 2 + c, x_partner(step, x, c) * 2 + c) for x in range(4) for c in range(2)]
    )


def shift(x, axis, k):
    n = {"x": 4, "y": 4}[axis]
    return lax.ppermute(x, axis, [(i, (i + k) % n) for i in range(n)])


def forward(x, k):
    pairs = [(y * 2 + c, (y + k * (1 - 2 * c)) % 4 * 2 + c) for y in range(4) for c in range(2)]
    return lax.ppermute(x, ("y", "c"), pairs)


def swap_core(x):
    return lax.ppermute(x, "c", [(0, 1), (1, 0)])


def ring_gather(h0, h1, axis, first=None):
    below0, above1 = shift(h0, axis, 1), shift(h1, axis, -1)
    below1, above0 = shift(h1, axis, 1), shift(h0, axis, -1)
    far = shift(below0, axis, 1), shift(above1, axis, -1)
    if first is not None:
        below1, above0, first = lax.optimization_barrier((below1, above0, first))
    return (below0, below1), (above0, above1), far, first


def place_kernel(rs, place, *refs):
    parts, out, sems = refs[: len(rs)], refs[-2], refs[-1]
    copies = []
    for i, (part, (r, h)) in enumerate(zip(parts, rs)):
        for j in range(4):
            row = lax.rem(place[0] + r + 2 * (r % 2) * place[2], 4) * TILE + place[4 + 4 * h + j] * BLOCK
            rows = out.at[pl.ds(pl.multiple_of(row, BLOCK), BLOCK)]
            copies.append(pltpu.make_async_copy(part.at[pl.ds(j * BLOCK, BLOCK)], rows, sems.at[4 * i + j]))
    for copy in copies:
        copy.start()
    for copy in copies:
        copy.wait()


def put_rows(place, parts, rs, to=None):
    whole = [pl.BlockSpec(memory_space=pltpu.VMEM)] * len(parts)
    return pl.pallas_call(
        functools.partial(place_kernel, rs),
        out_shape=jax.ShapeDtypeStruct((1024, D), BF16),
        in_specs=[pl.BlockSpec(memory_space=pltpu.SMEM)] + whole + [pl.BlockSpec(memory_space=pl.ANY)] * (to is not None),
        out_specs=pl.BlockSpec(memory_space=pl.ANY),
        scratch_shapes=[pltpu.SemaphoreType.DMA((4 * len(parts),))],
        input_output_aliases={} if to is None else {len(parts) + 1: 0},
        compiler_params=pltpu.CompilerParams(vmem_limit_bytes=16 << 20),
        cost_estimate=pl.CostEstimate(flops=0, bytes_accessed=4 * 128 * len(parts) * D, transcendentals=0),
        name="put_rows",
    )(place, *parts, *([] if to is None else [to]))


def score_kernel(n, others, *refs):
    es, f, stats = refs[:n], refs[n], refs[n + 1 : n + 1 + others]
    p_ref, top_ref, stat_ref, top_acc, sum_acc = refs[n + 1 + others :]
    t = pl.program_id(0)
    rows = jnp.concatenate([e[...] for e in es], axis=0)
    s = lax.dot_general(f[...], rows, ROW_DOT, preferred_element_type=F32)
    top = jnp.max(s, axis=0, keepdims=True)
    p = jnp.exp((s - top) * SCALE)
    p_ref[...] = p
    total = jnp.sum(p, axis=0, keepdims=True)

    @pl.when(t == 0)
    def _():
        top_ref[:1, :] = top
        top_acc[...] = top
        sum_acc[...] = total

    @pl.when(t == 1)
    def _():
        top_ref[1:, :] = top
        old = top_acc[...]
        new = jnp.maximum(old, top)
        l = sum_acc[...] * jnp.exp((old - new) * SCALE) + total * jnp.exp((top - new) * SCALE)
        stat = []
        for at in range(0, rows.shape[0], 256):
            for v in (new, l):
                stat += [v[:, at : at + ROWS], v[:, at + ROWS : at + 256]]
        stat = jnp.concatenate(stat, axis=0)
        if stats:
            own, near = stats
            stat = jnp.concatenate([own[...], near[:4, :], stat, near[4:, :]], axis=0)
            for i in range(8):
                stat_ref[i] = stat
        else:
            stat_ref[...] = stat


def scores(es, f, *stats):
    rows = sum(e.shape[0] for e in es)
    whole = lambda *shape: pl.BlockSpec(shape, lambda t: (0,) * len(shape))
    stat = (8, 16, ROWS) if stats else (rows // 64, ROWS)
    return pl.pallas_call(
        functools.partial(score_kernel, len(es), len(stats)),
        grid=(2,),
        in_specs=[whole(*e.shape) for e in es]
        + [pl.BlockSpec((512, D), lambda t: (t, 0))]
        + [whole(*v.shape) for v in stats],
        out_specs=[pl.BlockSpec((512, rows), lambda t: (t, 0)), whole(2, rows), whole(*stat)],
        out_shape=[
            jax.ShapeDtypeStruct((1024, rows), F32),
            jax.ShapeDtypeStruct((2, rows), F32),
            jax.ShapeDtypeStruct(stat, F32),
        ],
        scratch_shapes=[pltpu.VMEM((1, rows), F32), pltpu.VMEM((1, rows), F32)],
        compiler_params=pltpu.CompilerParams(vmem_limit_bytes=58 << 20),
        cost_estimate=pl.CostEstimate(flops=2 * 1024 * rows * D, bytes_accessed=6 << 20, transcendentals=1024 * rows),
        name="fine_scores",
    )(*es, f, *stats)


def find_factors(place, tops, stats, factors):
    x, c = place[1], place[2]
    for r in range(4):
        for d in range(2):
            ms, ls = [], []
            for src in range(8):
                sr = lax.rem(x + (r + 4 - src // 2), 4)
                sd = jnp.bitwise_xor(c, d ^ (src % 2))
                at = sr * 4 + sd
                ms.append(stats[src, pl.ds(at, 1), :])
                ls.append(stats[src, pl.ds(at + 2, 1), :])
            top = ms[0]
            for m in ms[1:]:
                top = jnp.maximum(top, m)
            total = jnp.zeros_like(top)
            for m, l in zip(ms, ls):
                total = total + l * jnp.exp((m - top) * SCALE)
            call, at = CALL_OF[r]
            at += d * ROWS
            to = (FIRST_BLOCK[r] + d) * ROWS
            factors[:, to : to + ROWS] = jnp.exp((tops[call][:, at : at + ROWS] - top) * SCALE) / total


def tile_sums(place, tile, factors, ps, es):
    out = jnp.zeros((TILE, D), F32)
    mass = jnp.zeros((TILE, 128), F32)
    at, k = 0, 0
    for p in ps:
        cols = p.shape[1]
        blocks = [p[pl.ds(pl.multiple_of(place[4 + j] * BLOCK, BLOCK), BLOCK), :] for j in range(8)]
        w = (jnp.concatenate(blocks, axis=0) * factors[pl.ds(tile // 2, 1), at : at + cols]).astype(BF16)
        rows = []
        while sum(e.shape[0] for e in rows) < cols:
            rows.append(es[k][...])
            k += 1
        out = out + jnp.dot(w, jnp.concatenate(rows, axis=0), preferred_element_type=F32)
        mass = mass + jnp.dot(w, jnp.ones((cols, 128), BF16), preferred_element_type=F32)
        at += cols
    return out, mass


def put_halves(out, mass, keep, keep_mass, send):
    keep[...] = out[:128]
    keep_mass[...] = mass[:128]
    send[:, :D] = out[128:].astype(BF16)
    high = mass[128:].astype(BF16).astype(F32)
    lane = lax.broadcasted_iota(jnp.int32, (128, 128), 1)
    send[:, D:] = jnp.where(lane < 64, high, mass[128:] - high).astype(BF16)


def first_kernel(n, place, *refs):
    es, ps, tops, stats = refs[:n], refs[n : n + 3], refs[n + 3 : n + 6], refs[n + 6]
    outs, factors = refs[n + 7 : n + 13], refs[n + 13]
    t = pl.program_id(0)

    @pl.when(t == 0)
    def _():
        find_factors(place, tops, stats, factors)

    out, mass = tile_sums(place, first_tile(t, place), factors, ps, es)
    for i in range(2):

        @pl.when(t == i)
        def _():
            put_halves(out, mass, *outs[3 * i : 3 * i + 3])


def rest_kernel(n, place, *refs):
    es, ps, factors, outs = refs[:n], refs[n : n + 3], refs[n + 3], refs[n + 4 :]
    t = pl.program_id(0)
    out, mass = tile_sums(place, rest_tile(t, place), factors, ps, es)
    for i in range(2):

        @pl.when(t == i)
        def _():
            put_halves(out, mass, *outs[3 * i : 3 * i + 3])


def first_tile(t, place):
    return lax.rem(place[0] + 2 - t, 4)


def rest_tile(t, place):
    return lax.rem(place[0] + 3 + t, 4)


def fine_sums(place, es, ps, tops, stats):
    whole = lambda *shape: pl.BlockSpec(shape, lambda t, s: (0,) * len(shape))
    halves = [
        jax.ShapeDtypeStruct((128, D), F32),
        jax.ShapeDtypeStruct((128, 128), F32),
        jax.ShapeDtypeStruct((128, WIDE), BF16),
    ]
    specs = [whole(*half.shape) for half in halves]
    params = pltpu.CompilerParams(vmem_limit_bytes=58 << 20)
    *first, factors = pl.pallas_call(
        functools.partial(first_kernel, len(es)),
        grid_spec=pltpu.PrefetchScalarGridSpec(
            num_scalar_prefetch=1,
            grid=(2,),
            in_specs=[whole(*e.shape) for e in es]
            + [pl.BlockSpec((TILE, p.shape[1]), lambda t, s: (first_tile(t, s), 0)) for p in ps]
            + [whole(*top.shape) for top in tops]
            + [whole(8, 16, ROWS)],
            out_specs=specs * 2 + [whole(2, 1024)],
        ),
        out_shape=halves * 2 + [jax.ShapeDtypeStruct((2, 1024), F32)],
        compiler_params=params,
        cost_estimate=pl.CostEstimate(flops=2 * 512 * 1024 * D, bytes_accessed=5 << 20, transcendentals=0),
        name="first_sums",
    )(place, *es, *ps, *tops, stats)
    rest = pl.pallas_call(
        functools.partial(rest_kernel, len(es)),
        grid_spec=pltpu.PrefetchScalarGridSpec(
            num_scalar_prefetch=1,
            grid=(2,),
            in_specs=[whole(*e.shape) for e in es]
            + [pl.BlockSpec((TILE, p.shape[1]), lambda t, s: (rest_tile(t, s), 0)) for p in ps]
            + [whole(2, 1024)],
            out_specs=specs * 2,
        ),
        out_shape=halves * 2,
        compiler_params=params,
        cost_estimate=pl.CostEstimate(flops=2 * 512 * 1024 * D, bytes_accessed=10 << 20, transcendentals=0),
        name="rest_sums",
    )(place, *es, *ps, factors)
    return first[:3], first[3:], rest[:3], rest[3:]


def load(ref, at, n):
    if isinstance(ref, tuple):
        return ref[0][at : at + n, :], ref[1][at : at + n, :]
    mass = ref[at : at + n, D:].astype(F32)
    mass = mass[:, :1] + mass[:, 64:65]
    return ref[at : at + n, :D].astype(F32), jnp.broadcast_to(mass, (n, 128))


def add(a, b):
    return a[0] + b[0], a[1] + b[1]


def store(ref, v):
    sums, mass = v
    ref[:, :D] = sums.astype(BF16)
    high = mass.astype(BF16).astype(F32)
    lane = lax.broadcasted_iota(jnp.int32, mass.shape, 1)
    ref[:, D:] = jnp.where(lane < 64, high, mass - high).astype(BF16)


def far_step(keep, mass, got, low, high):
    for at, out in ((0, low), (64, high)):
        store(out, add(load((keep, mass), at, 64), load(got, at, 64)))


def side_step(first, keep, mass, got, far, out):
    for at in (0, 64):
        v = add(load((keep, mass), at, 64), load(got, at, 64))
        if at == first:
            v = add(v, load(far, 0, 64))
        store(out.at[pl.ds(at, 64)], v)


def own_step(keep, mass, got, up, down, sums, masses, send):
    for at in (0, 64):
        v = add(load((keep, mass), at, 64), load(got, at, 64))
        v = add(v, add(load(up, at, 64), load(down, at, 64)))
        if at:
            store(send, v)
        else:
            sums[...], masses[...] = v


def half_step(keep, mass, got, out):
    store(out, add(load((keep, mass), 0, 64), load(got, 0, 64)))


def last_step(own, got, out):
    sums, mass = add(load(own, 0, 64), load(got, 0, 64))
    out[...] = (sums / jnp.maximum(mass[:, :1], 1.0)).astype(BF16)


def step(kernel, args, outs):
    whole = pl.BlockSpec(memory_space=pltpu.VMEM)
    out = pl.pallas_call(
        kernel,
        in_specs=[whole] * len(args),
        out_specs=[whole] * len(outs),
        out_shape=[jax.ShapeDtypeStruct(shape, t) for shape, t in outs],
        compiler_params=pltpu.CompilerParams(vmem_limit_bytes=16 << 20),
        cost_estimate=pl.CostEstimate(flops=1 << 20, bytes_accessed=2 << 20, transcendentals=0),
        name="add_" + getattr(kernel, "func", kernel).__name__,
    )(*args)
    return out if len(out) > 1 else out[0]


def coarse_kernel(place, s, top, total, fine, keep, send, m_keep):
    w = (jnp.exp(s[...] - top[...]) / total[...]).astype(BF16)
    out = jnp.dot(w, fine[...], preferred_element_type=F32)
    weight = lax.dot_general(jnp.ones((8, 1024), BF16), w, ROW_DOT, preferred_element_type=F32)[:1, :]
    first = place[2] == 0
    keep[0] = jnp.where(first, out[:128], out[128:])
    send[0, :128] = jnp.where(first, out[128:], out[:128]).astype(BF16)
    m_keep[0] = jnp.where(first, weight[:, :128], weight[:, 128:])
    sent = jnp.where(first, weight[:, 128:], weight[:, :128])
    high = sent.astype(BF16)
    low = (sent - high.astype(F32)).astype(BF16)
    send[0, 128:, :256] = jnp.broadcast_to(jnp.concatenate([high, low], axis=1), (EXTRA, 256))
    send[0, 128:, 256:] = jnp.zeros((EXTRA, D - 256), BF16)


def coarse_sums(place, s, top, total, fine):
    whole = lambda *shape: pl.BlockSpec(shape, lambda r, p: (0,) * len(shape))
    row = lambda *shape: pl.BlockSpec((1, *shape), lambda r, p: (r, 0, 0))
    swapped = pl.BlockSpec((1, 128 + EXTRA, D), lambda r, p: (p[16 + r], 0, 0))
    return pl.pallas_call(
        coarse_kernel,
        grid_spec=pltpu.PrefetchScalarGridSpec(
            num_scalar_prefetch=1,
            grid=(4,),
            in_specs=[pl.BlockSpec((256, 1024), lambda r, p: (p[12 + r], 0))]
            + [whole(1, 1024), whole(1, 1024), whole(1024, D)],
            out_specs=[row(128, D), swapped, row(1, 128)],
        ),
        out_shape=[
            jax.ShapeDtypeStruct((4, 128, D), F32),
            jax.ShapeDtypeStruct((4, 128 + EXTRA, D), BF16),
            jax.ShapeDtypeStruct((4, 1, 128), F32),
        ],
        compiler_params=pltpu.CompilerParams(vmem_limit_bytes=24 << 20),
        cost_estimate=pl.CostEstimate(flops=2 * 1024 * 1024 * D, bytes_accessed=12 << 20, transcendentals=1 << 20),
        name="coarse_sums",
    )(place, s, top, total, fine)


def split(v):
    high = lax.reduce_precision(v, 8, 7)
    return high, lax.reduce_precision(v - high, 8, 7)


def with_mass(total, mass, extra=EXTRA):
    rows = jnp.concatenate(split(mass), axis=1)
    rows = jnp.pad(rows, ((0, extra - rows.shape[0]), (0, total.shape[1] - rows.shape[1])))
    return jnp.concatenate([total, rows], axis=0).astype(BF16)


def coarse_scores(fine, coarse):
    s = lax.dot_general(coarse, fine, ROW_DOT, preferred_element_type=F32) * SCALE
    top = jnp.max(s, axis=0, keepdims=True)
    return s, top, jnp.sum(jnp.exp(s - top), axis=0, keepdims=True)


def coarse_rows(keep, send, m_keep):
    got = swap_core(send).astype(F32)
    total = keep + got[:, :128]
    mass = m_keep[:, 0] + got[:, 128, :128] + got[:, 128, 128:256]
    for step, n in ((0, 2), (1, 1)):
        got = x_exchange(with_mass(total[n:].reshape(n * 128, D), mass[n:], 8), step).astype(F32)
        total = total[:n] + got[: n * 128].reshape(n, 128, D)
        mass = mass[:n] + got[n * 128 : n * 128 + n, :128] + got[n * 128 : n * 128 + n, 128:256]
    return (total[0] / jnp.maximum(mass[0], 1.0)[:, None]).astype(BF16)


def shards(embeddings, fine, coarse):
    y, z, x, c = (lax.axis_index(a) for a in ("y", "z", "x", "c"))
    z_order = lax.dynamic_index_in_dim(jnp.asarray(Z_ORDER), z * 2 + c, 0, keepdims=False)
    x_places = lax.dynamic_index_in_dim(jnp.asarray(X_ORDER), x * 2 + c, 0, keepdims=False)
    place = jnp.concatenate([jnp.stack([y, x, c, z]), z_order, x_places])

    mine = [embeddings, swap_core(embeddings)]
    own = scores(mine, fine)
    below, above, far, own = ring_gather(embeddings[:HALF], embeddings[HALF:], "x", own)
    near = [*above, *map(swap_core, above), *below, *map(swap_core, below)]
    far = [*far, *map(swap_core, far)]
    calls = [own, scores(near, fine)]
    calls.append(scores(far, fine, calls[0][2], calls[1][2]))
    stats = lax.all_to_all(calls[2][2], ("x", "c"), 0, 0)
    far, up, down, own = fine_sums(
        place, [*mine, *near, *far], [call[0] for call in calls], [call[1] for call in calls], stats
    )

    sent = lambda n: ((n, WIDE), BF16)
    got, got_up = exchange(far[2], 0), exchange(up[2], 0)
    (down, own), got = lax.optimization_barrier(((down, own), got))
    got_down, got_own = exchange(down[2], 0), exchange(own[2], 0)
    far0, far1 = step(far_step, [far[0], far[1], got], [sent(64), sent(64)])
    far0, far1 = shift(far0, "y", 1), shift(far1, "y", -1)
    up = step(functools.partial(side_step, 0), [up[0], up[1], got_up, far0], [sent(128)])
    down = step(functools.partial(side_step, 64), [down[0], down[1], got_down, far1], [sent(128)])
    got_own, coarse = lax.optimization_barrier((got_own, coarse))
    c_sums = coarse_sums(place, *coarse_scores(fine, coarse), fine)
    up, down = shift(up, "y", 1), shift(down, "y", -1)
    up, down, c_sums = lax.optimization_barrier((up, down, c_sums))
    sums, masses, send = step(
        own_step, [own[0], own[1], got_own, up, down], [((64, D), F32), ((64, 128), F32), sent(64)]
    )

    own = step(half_step, [sums, masses, exchange(send, 1)], [sent(64)])
    a = step(last_step, [own, exchange(own, 2)], [((64, D), BF16)])

    a0 = jnp.concatenate([a, exchange(a, 1)], axis=0)
    a1 = exchange(a0, 0)
    back0, next0 = forward(a0, 1), forward(a0, -1)
    a1, back0, next0 = lax.optimization_barrier((a1, back0, next0))
    next1, back1 = forward(a1, -1), forward(a1, 1)
    far0, far1 = forward(back0, 1), forward(next1, -1)
    new_fine = put_rows(place, [a0, a1, next0, back0], [(0, 0), (0, 1), (1, 0), (3, 0)])
    new_coarse = coarse_rows(*c_sums)
    far1, new_coarse, new_fine = lax.optimization_barrier((far1, new_coarse, new_fine))
    new_fine = put_rows(place, [next1, far0, far1, back1], [(1, 1), (2, 0), (2, 1), (3, 1)], new_fine)
    return new_fine, new_coarse


def solution(mesh):
    torus = Mesh(mesh.devices.reshape(4, 8, 4, 2), ("y", "z", "x", "c"))
    return jax.shard_map(
        shards,
        mesh=torus,
        in_specs=(P(("y", "z", "x", "c"), None), P(("x", "c"), None), P()),
        out_specs=(P(("x", "c"), None), P(("x", "c"), None)),
        check_vma=False,
    )
```

```python
import functools
import math

import jax
import jax.numpy as jnp
import numpy as np
from jax import lax
from jax.experimental import pallas as pl
from jax.experimental.pallas import tpu as pltpu
from jax.sharding import Mesh, PartitionSpec as P

D = 1536
ROWS = 128
HALF = ROWS // 2
BLOCK = 32
TILE = 8 * BLOCK
EXTRA = 16
WIDE = D + 128
CALL_OF = ((0, 0), (1, 0), (2, 0), (1, 2 * ROWS))
FIRST_BLOCK = (0, 2, 6, 4)
SCALE = 4.0 / math.sqrt(D)
BF16, F32 = jnp.bfloat16, jnp.float32
ROW_DOT = (((1,), (1,)), ((), ()))

Z_PAIRS = ((1, 0, 3, 2, 5, 4, 7, 6), (7, 2, 1, 4, 3, 6, 5, 0), (3, 6, 5, 0, 7, 2, 1, 4))


def partner(step, z, c):
    return (Z_PAIRS[step][(z - c) % 8] + c) % 8


def order(step, z, c):
    if step == 2:
        return sorted((z, partner(2, z, c)))
    return order(step + 1, z, c) + order(step + 1, partner(step, z, c), c)


X_PAIRS = ((1, 0, 3, 2), (3, 2, 1, 0))


def x_partner(step, x, c):
    return (X_PAIRS[step][(x - c) % 4] + c) % 4


def x_order(step, x, c):
    if step == 2:
        return [x]
    return x_order(step + 1, x, c) + x_order(step + 1, x_partner(step, x, c), c)


X_ORDER = np.array(
    [
        x_order(0, x, c) + [x_order(0, x, 1 - c).index(i) for i in x_order(0, x, c)]
        for x in range(4)
        for c in range(2)
    ],
    np.int32,
)
Z_ORDER = np.array([order(0, z, c) for z in range(8) for c in range(2)], np.int32)


def exchange(x, step):
    return lax.ppermute(x, ("z", "c"), [(z * 2 + c, partner(step, z, c) * 2 + c) for z in range(8) for c in range(2)])


def x_exchange(v, step):
    return lax.ppermute(
        v, ("x", "c"), [(x * 2 + c, x_partner(step, x, c) * 2 + c) for x in range(4) for c in range(2)]
    )


def shift(x, axis, k):
    n = {"x": 4, "y": 4}[axis]
    return lax.ppermute(x, axis, [(i, (i + k) % n) for i in range(n)])


def forward(x, k):
    pairs = [(y * 2 + c, (y + k * (1 - 2 * c)) % 4 * 2 + c) for y in range(4) for c in range(2)]
    return lax.ppermute(x, ("y", "c"), pairs)


def swap_core(x):
    return lax.ppermute(x, "c", [(0, 1), (1, 0)])


def ring_gather(h0, h1, axis, first=None):
    below0, above1 = shift(h0, axis, 1), shift(h1, axis, -1)
    below1, above0 = shift(h1, axis, 1), shift(h0, axis, -1)
    far = shift(below0, axis, 1), shift(above1, axis, -1)
    if first is not None:
        below1, above0, first = lax.optimization_barrier((below1, above0, first))
    return (below0, below1), (above0, above1), far, first


def place_kernel(rs, place, *refs):
    parts, out, sems = refs[: len(rs)], refs[-2], refs[-1]
    copies = []
    for part, (r, first) in zip(parts, rs):
        for j in range(part.shape[0] // BLOCK):
            at = lax.rem(place[0] + r + 2 * (r % 2) * place[2], 4) * TILE + place[4 + first + j] * BLOCK
            rows = out.at[pl.ds(pl.multiple_of(at, BLOCK), BLOCK)]
            copies.append(pltpu.make_async_copy(part.at[pl.ds(j * BLOCK, BLOCK)], rows, sems.at[len(copies)]))
    for copy in copies:
        copy.start()
    for copy in copies:
        copy.wait()


def put_rows(place, parts, rs, to=None):
    whole = [pl.BlockSpec(memory_space=pltpu.VMEM)] * len(parts)
    return pl.pallas_call(
        functools.partial(place_kernel, rs),
        out_shape=jax.ShapeDtypeStruct((1024, D), BF16),
        in_specs=[pl.BlockSpec(memory_space=pltpu.SMEM)] + whole + [pl.BlockSpec(memory_space=pl.ANY)] * (to is not None),
        out_specs=pl.BlockSpec(memory_space=pl.ANY),
        scratch_shapes=[pltpu.SemaphoreType.DMA((sum(part.shape[0] for part in parts) // BLOCK,))],
        input_output_aliases={} if to is None else {len(parts) + 1: 0},
        compiler_params=pltpu.CompilerParams(vmem_limit_bytes=16 << 20),
        cost_estimate=pl.CostEstimate(flops=0, bytes_accessed=4 * 128 * len(parts) * D, transcendentals=0),
        name="put_rows",
    )(place, *parts, *([] if to is None else [to]))


def score_kernel(n, others, *refs):
    es, f, stats = refs[:n], refs[n], refs[n + 1 : n + 1 + others]
    p_ref, top_ref, stat_ref, top_acc, sum_acc = refs[n + 1 + others :]
    t = pl.program_id(0)
    rows = jnp.concatenate([e[...] for e in es], axis=0)
    s = lax.dot_general(f[...], rows, ROW_DOT, preferred_element_type=F32)
    top = jnp.max(s, axis=0, keepdims=True)
    p = jnp.exp((s - top) * SCALE)
    p_ref[...] = p
    total = jnp.sum(p, axis=0, keepdims=True)

    @pl.when(t == 0)
    def _():
        top_ref[:1, :] = top
        top_acc[...] = top
        sum_acc[...] = total

    @pl.when(t == 1)
    def _():
        top_ref[1:, :] = top
        old = top_acc[...]
        new = jnp.maximum(old, top)
        l = sum_acc[...] * jnp.exp((old - new) * SCALE) + total * jnp.exp((top - new) * SCALE)
        stat = []
        for at in range(0, rows.shape[0], 256):
            for v in (new, l):
                stat += [v[:, at : at + ROWS], v[:, at + ROWS : at + 256]]
        stat = jnp.concatenate(stat, axis=0)
        if stats:
            own, near = stats
            stat = jnp.concatenate([own[...], near[:4, :], stat, near[4:, :]], axis=0)
            for i in range(8):
                stat_ref[i] = stat
        else:
            stat_ref[...] = stat


def scores(es, f, *stats):
    rows = sum(e.shape[0] for e in es)
    whole = lambda *shape: pl.BlockSpec(shape, lambda t: (0,) * len(shape))
    stat = (8, 16, ROWS) if stats else (rows // 64, ROWS)
    return pl.pallas_call(
        functools.partial(score_kernel, len(es), len(stats)),
        grid=(2,),
        in_specs=[whole(*e.shape) for e in es]
        + [pl.BlockSpec((512, D), lambda t: (t, 0))]
        + [whole(*v.shape) for v in stats],
        out_specs=[pl.BlockSpec((512, rows), lambda t: (t, 0)), whole(2, rows), whole(*stat)],
        out_shape=[
            jax.ShapeDtypeStruct((1024, rows), F32),
            jax.ShapeDtypeStruct((2, rows), F32),
            jax.ShapeDtypeStruct(stat, F32),
        ],
        scratch_shapes=[pltpu.VMEM((1, rows), F32), pltpu.VMEM((1, rows), F32)],
        compiler_params=pltpu.CompilerParams(vmem_limit_bytes=58 << 20),
        cost_estimate=pl.CostEstimate(flops=2 * 1024 * rows * D, bytes_accessed=6 << 20, transcendentals=1024 * rows),
        name="fine_scores",
    )(*es, f, *stats)


def find_factors(place, tops, stats, factors):
    x, c = place[1], place[2]
    for r in range(4):
        for d in range(2):
            ms, ls = [], []
            for src in range(8):
                sr = lax.rem(x + (r + 4 - src // 2), 4)
                sd = jnp.bitwise_xor(c, d ^ (src % 2))
                at = sr * 4 + sd
                ms.append(stats[src, pl.ds(at, 1), :])
                ls.append(stats[src, pl.ds(at + 2, 1), :])
            top = ms[0]
            for m in ms[1:]:
                top = jnp.maximum(top, m)
            total = jnp.zeros_like(top)
            for m, l in zip(ms, ls):
                total = total + l * jnp.exp((m - top) * SCALE)
            call, at = CALL_OF[r]
            at += d * ROWS
            to = (FIRST_BLOCK[r] + d) * ROWS
            factors[:, to : to + ROWS] = jnp.exp((tops[call][:, at : at + ROWS] - top) * SCALE) / total


def tile_sums(place, tile, factors, ps, es):
    out = jnp.zeros((TILE, D), F32)
    mass = jnp.zeros((TILE, 128), F32)
    at, k = 0, 0
    for p in ps:
        cols = p.shape[1]
        blocks = [p[pl.ds(pl.multiple_of(place[4 + j] * BLOCK, BLOCK), BLOCK), :] for j in range(8)]
        w = (jnp.concatenate(blocks, axis=0) * factors[pl.ds(tile // 2, 1), at : at + cols]).astype(BF16)
        rows = []
        while sum(e.shape[0] for e in rows) < cols:
            rows.append(es[k][...])
            k += 1
        out = out + jnp.dot(w, jnp.concatenate(rows, axis=0), preferred_element_type=F32)
        mass = mass + jnp.dot(w, jnp.ones((cols, 128), BF16), preferred_element_type=F32)
        at += cols
    return out, mass


def put_halves(out, mass, keep, keep_mass, send):
    keep[...] = out[:128]
    keep_mass[...] = mass[:128]
    send[:, :D] = out[128:].astype(BF16)
    high = mass[128:].astype(BF16).astype(F32)
    lane = lax.broadcasted_iota(jnp.int32, (128, 128), 1)
    send[:, D:] = jnp.where(lane < 64, high, mass[128:] - high).astype(BF16)


def first_kernel(n, place, *refs):
    es, ps, tops, stats = refs[:n], refs[n : n + 3], refs[n + 3 : n + 6], refs[n + 6]
    outs, factors = refs[n + 7 : n + 13], refs[n + 13]
    t = pl.program_id(0)

    @pl.when(t == 0)
    def _():
        find_factors(place, tops, stats, factors)

    out, mass = tile_sums(place, first_tile(t, place), factors, ps, es)
    for i in range(2):

        @pl.when(t == i)
        def _():
            put_halves(out, mass, *outs[3 * i : 3 * i + 3])


def rest_kernel(n, place, *refs):
    es, ps, factors, outs = refs[:n], refs[n : n + 3], refs[n + 3], refs[n + 4 :]
    t = pl.program_id(0)
    out, mass = tile_sums(place, rest_tile(t, place), factors, ps, es)
    for i in range(2):

        @pl.when(t == i)
        def _():
            put_halves(out, mass, *outs[3 * i : 3 * i + 3])


def first_tile(t, place):
    return lax.rem(place[0] + 2 - t, 4)


def rest_tile(t, place):
    return lax.rem(place[0] + 3 + t, 4)


def fine_sums(place, es, ps, tops, stats):
    whole = lambda *shape: pl.BlockSpec(shape, lambda t, s: (0,) * len(shape))
    halves = [
        jax.ShapeDtypeStruct((128, D), F32),
        jax.ShapeDtypeStruct((128, 128), F32),
        jax.ShapeDtypeStruct((128, WIDE), BF16),
    ]
    specs = [whole(*half.shape) for half in halves]
    params = pltpu.CompilerParams(vmem_limit_bytes=58 << 20)
    *first, factors = pl.pallas_call(
        functools.partial(first_kernel, len(es)),
        grid_spec=pltpu.PrefetchScalarGridSpec(
            num_scalar_prefetch=1,
            grid=(2,),
            in_specs=[whole(*e.shape) for e in es]
            + [pl.BlockSpec((TILE, p.shape[1]), lambda t, s: (first_tile(t, s), 0)) for p in ps]
            + [whole(*top.shape) for top in tops]
            + [whole(8, 16, ROWS)],
            out_specs=specs * 2 + [whole(2, 1024)],
        ),
        out_shape=halves * 2 + [jax.ShapeDtypeStruct((2, 1024), F32)],
        compiler_params=params,
        cost_estimate=pl.CostEstimate(flops=2 * 512 * 1024 * D, bytes_accessed=5 << 20, transcendentals=0),
        name="first_sums",
    )(place, *es, *ps, *tops, stats)
    rest = pl.pallas_call(
        functools.partial(rest_kernel, len(es)),
        grid_spec=pltpu.PrefetchScalarGridSpec(
            num_scalar_prefetch=1,
            grid=(2,),
            in_specs=[whole(*e.shape) for e in es]
            + [pl.BlockSpec((TILE, p.shape[1]), lambda t, s: (rest_tile(t, s), 0)) for p in ps]
            + [whole(2, 1024)],
            out_specs=specs * 2,
        ),
        out_shape=halves * 2,
        compiler_params=params,
        cost_estimate=pl.CostEstimate(flops=2 * 512 * 1024 * D, bytes_accessed=10 << 20, transcendentals=0),
        name="rest_sums",
    )(place, *es, *ps, factors)
    return first[:3], first[3:], rest[:3], rest[3:]


def load(ref, at, n):
    if isinstance(ref, tuple):
        return ref[0][at : at + n, :], ref[1][at : at + n, :]
    mass = ref[at : at + n, D:].astype(F32)
    mass = mass[:, :1] + mass[:, 64:65]
    return ref[at : at + n, :D].astype(F32), jnp.broadcast_to(mass, (n, 128))


def add(a, b):
    return a[0] + b[0], a[1] + b[1]


def store(ref, v):
    sums, mass = v
    ref[:, :D] = sums.astype(BF16)
    high = mass.astype(BF16).astype(F32)
    lane = lax.broadcasted_iota(jnp.int32, mass.shape, 1)
    ref[:, D:] = jnp.where(lane < 64, high, mass - high).astype(BF16)


def far_step(keep, mass, got, low, high):
    for at, out in ((0, low), (64, high)):
        store(out, add(load((keep, mass), at, 64), load(got, at, 64)))


def side_step(first, keep, mass, got, far, out):
    for at in (0, 64):
        v = add(load((keep, mass), at, 64), load(got, at, 64))
        if at == first:
            v = add(v, load(far, 0, 64))
        store(out.at[pl.ds(at, 64)], v)


def own_step(keep, mass, got, up, down, sums, masses, send):
    for at in (0, 64):
        v = add(load((keep, mass), at, 64), load(got, at, 64))
        v = add(v, add(load(up, at, 64), load(down, at, 64)))
        if at:
            store(send, v)
        else:
            sums[...], masses[...] = v


def half_step(keep, mass, got, out):
    store(out, add(load((keep, mass), 0, 64), load(got, 0, 64)))


def last_step(own, got, out):
    sums, mass = add(load(own, 0, 64), load(got, 0, 64))
    out[...] = (sums / jnp.maximum(mass[:, :1], 1.0)).astype(BF16)


def step(kernel, args, outs):
    whole = pl.BlockSpec(memory_space=pltpu.VMEM)
    out = pl.pallas_call(
        kernel,
        in_specs=[whole] * len(args),
        out_specs=[whole] * len(outs),
        out_shape=[jax.ShapeDtypeStruct(shape, t) for shape, t in outs],
        compiler_params=pltpu.CompilerParams(vmem_limit_bytes=16 << 20),
        cost_estimate=pl.CostEstimate(flops=1 << 20, bytes_accessed=2 << 20, transcendentals=0),
        name="add_" + getattr(kernel, "func", kernel).__name__,
    )(*args)
    return out if len(out) > 1 else out[0]


def coarse_kernel(place, s, top, total, fine, keep, send, m_keep):
    w = (jnp.exp(s[...] - top[...]) / total[...]).astype(BF16)
    out = jnp.dot(w, fine[...], preferred_element_type=F32)
    weight = lax.dot_general(jnp.ones((8, 1024), BF16), w, ROW_DOT, preferred_element_type=F32)[:1, :]
    first = place[2] == 0
    keep[0] = jnp.where(first, out[:128], out[128:])
    send[0, :128] = jnp.where(first, out[128:], out[:128]).astype(BF16)
    m_keep[0] = jnp.where(first, weight[:, :128], weight[:, 128:])
    sent = jnp.where(first, weight[:, 128:], weight[:, :128])
    high = sent.astype(BF16)
    low = (sent - high.astype(F32)).astype(BF16)
    send[0, 128:, :256] = jnp.broadcast_to(jnp.concatenate([high, low], axis=1), (EXTRA, 256))
    send[0, 128:, 256:] = jnp.zeros((EXTRA, D - 256), BF16)


def coarse_sums(place, s, top, total, fine):
    whole = lambda *shape: pl.BlockSpec(shape, lambda r, p: (0,) * len(shape))
    row = lambda *shape: pl.BlockSpec((1, *shape), lambda r, p: (r, 0, 0))
    swapped = pl.BlockSpec((1, 128 + EXTRA, D), lambda r, p: (p[16 + r], 0, 0))
    return pl.pallas_call(
        coarse_kernel,
        grid_spec=pltpu.PrefetchScalarGridSpec(
            num_scalar_prefetch=1,
            grid=(4,),
            in_specs=[pl.BlockSpec((256, 1024), lambda r, p: (p[12 + r], 0))]
            + [whole(1, 1024), whole(1, 1024), whole(1024, D)],
            out_specs=[row(128, D), swapped, row(1, 128)],
        ),
        out_shape=[
            jax.ShapeDtypeStruct((4, 128, D), F32),
            jax.ShapeDtypeStruct((4, 128 + EXTRA, D), BF16),
            jax.ShapeDtypeStruct((4, 1, 128), F32),
        ],
        compiler_params=pltpu.CompilerParams(vmem_limit_bytes=24 << 20),
        cost_estimate=pl.CostEstimate(flops=2 * 1024 * 1024 * D, bytes_accessed=12 << 20, transcendentals=1 << 20),
        name="coarse_sums",
    )(place, s, top, total, fine)


def split(v):
    high = lax.reduce_precision(v, 8, 7)
    return high, lax.reduce_precision(v - high, 8, 7)


def with_mass(total, mass, extra=EXTRA):
    rows = jnp.concatenate(split(mass), axis=1)
    rows = jnp.pad(rows, ((0, extra - rows.shape[0]), (0, total.shape[1] - rows.shape[1])))
    return jnp.concatenate([total, rows], axis=0).astype(BF16)


def coarse_scores(fine, coarse):
    s = lax.dot_general(coarse, fine, ROW_DOT, preferred_element_type=F32) * SCALE
    top = jnp.max(s, axis=0, keepdims=True)
    return s, top, jnp.sum(jnp.exp(s - top), axis=0, keepdims=True)


def coarse_rows(keep, send, m_keep):
    got = swap_core(send).astype(F32)
    total = keep + got[:, :128]
    mass = m_keep[:, 0] + got[:, 128, :128] + got[:, 128, 128:256]
    for step, n in ((0, 2), (1, 1)):
        got = x_exchange(with_mass(total[n:].reshape(n * 128, D), mass[n:], 8), step).astype(F32)
        total = total[:n] + got[: n * 128].reshape(n, 128, D)
        mass = mass[:n] + got[n * 128 : n * 128 + n, :128] + got[n * 128 : n * 128 + n, 128:256]
    return (total[0] / jnp.maximum(mass[0], 1.0)[:, None]).astype(BF16)


def shards(embeddings, fine, coarse):
    y, z, x, c = (lax.axis_index(a) for a in ("y", "z", "x", "c"))
    z_order = lax.dynamic_index_in_dim(jnp.asarray(Z_ORDER), z * 2 + c, 0, keepdims=False)
    x_places = lax.dynamic_index_in_dim(jnp.asarray(X_ORDER), x * 2 + c, 0, keepdims=False)
    place = jnp.concatenate([jnp.stack([y, x, c, z]), z_order, x_places])

    mine = [embeddings, swap_core(embeddings)]
    own = scores(mine, fine)
    below, above, far, own = ring_gather(embeddings[:HALF], embeddings[HALF:], "x", own)
    near = [*above, *map(swap_core, above), *below, *map(swap_core, below)]
    far = [*far, *map(swap_core, far)]
    calls = [own, scores(near, fine)]
    calls.append(scores(far, fine, calls[0][2], calls[1][2]))
    stats = lax.all_to_all(calls[2][2], ("x", "c"), 0, 0)
    far, up, down, own = fine_sums(
        place, [*mine, *near, *far], [call[0] for call in calls], [call[1] for call in calls], stats
    )

    sent = lambda n: ((n, WIDE), BF16)
    got, got_up = exchange(far[2], 0), exchange(up[2], 0)
    (down, own), got = lax.optimization_barrier(((down, own), got))
    got_down, got_own = exchange(down[2], 0), exchange(own[2], 0)
    far0, far1 = step(far_step, [far[0], far[1], got], [sent(64), sent(64)])
    far0, far1 = shift(far0, "y", 1), shift(far1, "y", -1)
    up = step(functools.partial(side_step, 0), [up[0], up[1], got_up, far0], [sent(128)])
    down = step(functools.partial(side_step, 64), [down[0], down[1], got_down, far1], [sent(128)])
    got_own, coarse = lax.optimization_barrier((got_own, coarse))
    c_sums = coarse_sums(place, *coarse_scores(fine, coarse), fine)
    up, down = shift(up, "y", 1), shift(down, "y", -1)
    up, down, c_sums = lax.optimization_barrier((up, down, c_sums))
    sums, masses, send = step(
        own_step, [own[0], own[1], got_own, up, down], [((64, D), F32), ((64, 128), F32), sent(64)]
    )

    own = step(half_step, [sums, masses, exchange(send, 1)], [sent(64)])
    a = step(last_step, [own, exchange(own, 2)], [((64, D), BF16)])

    b = exchange(a, 1)
    back_a, next_a = forward(a, 1), forward(a, -1)
    a0 = jnp.concatenate([a, b], axis=0)
    a1 = exchange(a0, 0)
    back_b, next_b = forward(b, 1), forward(b, -1)
    far_a = forward(back_a, 1)
    a1, back_b, next_b = lax.optimization_barrier((a1, back_b, next_b))
    next1, back1 = forward(a1, -1), forward(a1, 1)
    far_b, far1 = forward(back_b, 1), forward(next1, -1)
    new_fine = put_rows(
        place, [a0, a1, next_a, next_b, back_a, back_b], [(0, 0), (0, 4), (1, 0), (1, 2), (3, 0), (3, 2)]
    )
    new_coarse = coarse_rows(*c_sums)
    far1, new_coarse, new_fine = lax.optimization_barrier((far1, new_coarse, new_fine))
    new_fine = put_rows(
        place, [next1, far_a, far_b, far1, back1], [(1, 4), (2, 0), (2, 2), (2, 4), (3, 4)], new_fine
    )
    return new_fine, new_coarse


def solution(mesh):
    torus = Mesh(mesh.devices.reshape(4, 8, 4, 2), ("y", "z", "x", "c"))
    return jax.shard_map(
        shards,
        mesh=torus,
        in_specs=(P(("y", "z", "x", "c"), None), P(("x", "c"), None), P()),
        out_specs=(P(("x", "c"), None), P(("x", "c"), None)),
        check_vma=False,
    )
```
